512 devices in a mesh: wn: 16 (over z_lo, core), sw: 32 (over z_hi, y, x).
Axes of the slice: x: 4, y: 4, z: 16 (z_hi: 2, z_lo: 8; z = z_hi * 8 + z_lo), core: 2. Of those that a mesh axis runs over, the one named last changes fastest.
Arguments:
- salinity: bfloat16 [6, 6144, 3072], P(None, ('wn', 'sw')), may hold values from -6 to 6
- velocity: bfloat16 [3, 2, 16, 128, 1024], P(None, None, None, 'sw', 'wn'), may hold values from -6 to 6
- wall_index: int32 [3072], replicated, may hold values from 0 to 1022, as said below
- wall_weight: float32 [3072], replicated, may hold values from 0 to 1
- spacing: float32 [3072], replicated, may hold values from 0.5 to 2
Outputs:
- salinity_new: bfloat16 [6, 6144, 3072], P(None, ('wn', 'sw'))
- coarse_salinity: bfloat16 [2, 16, 128, 1024], P(None, None, 'sw', 'wn')
The draws below stay inside these ranges and needn't reach their ends.
Inputs may be any that keep to these rules, and one draw needn't show every extreme that they name: `wall_index`: nondecreasing; the value 1024 - 2 occurs exactly 6 times, every other value between 1 and 5 times.
All inputs are finite; a program needn't handle non-finite values.
Results may differ from the reference program's by a relative error of at most 0.0039.
Values may be sent and summed in bfloat16 or wider, within the bound.
No kernel may reach another device: no remote copies, remote signals or barrier semaphores. Data moves between devices by JAX's collectives and lax.ppermute only.
A program may use at most 64 MiB of HBM per device.

```python
import math
import jax
import jax.numpy as jnp
from jax import lax

NXC = 1024
PZ = 2
NXF = 3072
PZF = 6
NYS = 128
NYC = 2048
NYF = 6144
N_WN = 16


def draw_wall_index(key, part):
    key = jax.random.fold_in(key, 7)
    pair_count = (NXC - 2) // 2
    offsets = jax.random.randint(key, (pair_count,), -2, 3)
    deltas = jnp.stack([offsets, -offsets], axis=1).reshape(-1)
    counts = jnp.concatenate([3 + deltas, jnp.full((NXC - 1 - 2 * pair_count,), 3, jnp.int32)]).astype(jnp.int32)
    counts = counts.at[-1].add(3)
    ends = jnp.cumsum(counts).astype(jnp.int32)
    positions = jnp.arange(3 * NXC, dtype=jnp.int32)
    return jnp.sum((ends[None, :] <= positions[:, None]).astype(jnp.int32), axis=1).astype(jnp.int32)


def block_scale(key, extent, shards, smallest, high):
    level, own = 1.0, jax.random.fold_in(key, 6)
    for position, shards_of in shards:
        steps = jnp.exp(jax.random.uniform(jax.random.fold_in(own, position), (shards_of,), jnp.float32, smallest / len(shards), high / len(shards)))
        level = level * jnp.repeat(steps, extent[position] // shards_of).reshape([-1 if axis == position else 1 for axis in range(len(extent))])
    return level


def gaussian(key, dims, deviation, reach, cuts=(), kind=jnp.bfloat16):
    entries = deviation * jax.random.normal(key, dims, jnp.float32)
    if cuts:
        entries = entries * block_scale(key, dims, cuts, -0.22, 0.18)
    return jnp.clip(entries, -reach, reach).astype(kind)


def setup_inputs(seed: int = 0) -> dict:
    splits = jax.random.split(jax.random.key(seed), 6)
    salinity = gaussian(splits[0], (PZF, NYF, NXF), 1.0, 6.0, ((1, 512),))
    velocity = gaussian(splits[1], (3, PZ, N_WN, NYS, NXC), 1.0, 6.0, ((3, 32), (4, 16)))
    wall_index = draw_wall_index(jax.random.fold_in(splits[5], 71), 0)
    wall_weight = jnp.clip(jax.random.uniform(splits[3], (NXF,), jnp.float32, 0.0, 1.0), 0.0, 1.0)
    spacing = jnp.clip(jnp.exp(jax.random.uniform(splits[4], (NXF,), jnp.float32, math.log(0.5), math.log(2.0))), 0.5, 2.0)
    return {"salinity": salinity, "velocity": velocity, "wall_index": wall_index, "wall_weight": wall_weight, "spacing": spacing}


time_step = 0.5
runge_gamma = 8.0 / 15.0
diffusivity = 0.3


def block_layout(coarse_count):
    window = min(coarse_count, 256)
    fine_width = 3 * min(coarse_count, 128)
    block_count = (3 * coarse_count) // fine_width
    starts = [min(max(b * fine_width // 3 - 64, 0), coarse_count - window) for b in range(block_count)]
    return window, fine_width, starts


def weight_block(wall_index, wall_weight, start, window, fine_start, fine_width):
    index_part = wall_index[fine_start:fine_start + fine_width]
    weight_part = wall_weight[fine_start:fine_start + fine_width]
    rows = start + jnp.arange(window, dtype=jnp.int32)
    lower_hit = (rows[:, None] == index_part[None, :]).astype(jnp.float32)
    upper_hit = (rows[:, None] == (index_part + 1)[None, :]).astype(jnp.float32)
    return lower_hit * (1.0 - weight_part)[None, :] + upper_hit * weight_part[None, :]


def wall_interpolate(values, wall_index, wall_weight):
    window, fine_width, starts = block_layout(values.shape[-1])
    pieces = []
    for number, start in enumerate(starts):
        matrix = weight_block(wall_index, wall_weight, start, window, number * fine_width, fine_width)
        pieces.append(jnp.einsum("cpyk,kj->cpyj", values[..., start:start + window], matrix, precision=lax.Precision.HIGHEST))
    return jnp.concatenate(pieces, axis=-1)


def wall_restrict(grouped, wall_index, wall_weight, coarse_count):
    window, fine_width, starts = block_layout(coarse_count)
    total = jnp.zeros(grouped.shape[:-1] + (coarse_count,), jnp.float32)
    for number, start in enumerate(starts):
        matrix = weight_block(wall_index, wall_weight, start, window, number * fine_width, fine_width)
        part = grouped[..., number * fine_width:(number + 1) * fine_width]
        total = total.at[..., start:start + window].add(jnp.einsum("pyj,kj->pyk", part, matrix, precision=lax.Precision.HIGHEST))
    return total


def fine_velocity(coarse_block, wall_index, wall_weight):
    values = coarse_block.astype(jnp.float32)
    normal = wall_interpolate(values, wall_index, wall_weight)
    center = normal[:, :, 1:-1]
    previous = normal[:, :, :-2]
    following = normal[:, :, 2:]
    one_third = 1.0 / 3.0
    streamwise = jnp.stack([one_third * previous + 2.0 * one_third * center, center, 2.0 * one_third * center + one_third * following], axis=3)
    block_shape = streamwise.shape
    streamwise = streamwise.reshape(block_shape[0], block_shape[1], block_shape[2] * 3, block_shape[4])
    plane_below = jnp.roll(streamwise, 1, axis=1)
    plane_above = jnp.roll(streamwise, -1, axis=1)
    across = jnp.stack([one_third * plane_below + 2.0 * one_third * streamwise, streamwise, 2.0 * one_third * streamwise + one_third * plane_above], axis=2)
    return across.reshape(block_shape[0], block_shape[1] * 3, block_shape[2] * 3, block_shape[4])


def advance(salinity_block, velocity_fine, spacing):
    field = salinity_block.astype(jnp.float32)
    middle = field[:, 1:-1]
    forward = field[:, 2:]
    behind = field[:, :-2]
    wall_low = jnp.concatenate([-middle[:, :, :1], middle[:, :, :-1]], axis=2)
    wall_high = jnp.concatenate([middle[:, :, 1:], -middle[:, :, -1:]], axis=2)
    span_low = jnp.roll(middle, 1, axis=0)
    span_high = jnp.roll(middle, -1, axis=0)
    centers = 0.5 * (spacing[:-1] + spacing[1:])
    gap_low = jnp.concatenate([spacing[:1], centers])
    gap_high = jnp.concatenate([centers, spacing[-1:]])
    slope = (wall_high - wall_low) / (gap_low + gap_high)
    curvature = ((wall_high - middle) / gap_high - (middle - wall_low) / gap_low) / spacing
    laplace = curvature + (forward - 2.0 * middle + behind) + (span_high - 2.0 * middle + span_low)
    transport = velocity_fine[0] * 0.5 * (forward - behind) + velocity_fine[1] * slope + velocity_fine[2] * 0.5 * (span_high - span_low)
    return (middle + time_step * runge_gamma * (diffusivity * laplace - transport)).astype(jnp.bfloat16)


def restrict(updated, wall_index, wall_weight):
    values = updated.astype(jnp.float32)
    plane_count, row_count, cell_count = updated.shape
    grouped = values.reshape(plane_count // 3, 3, row_count // 3, 3, cell_count).sum(axis=(1, 3)) / 3.0
    total = wall_restrict(grouped, wall_index, wall_weight, cell_count // 3)
    return (total / 3.0).astype(jnp.bfloat16)


def reference(salinity, velocity, wall_index, wall_weight, spacing):
    components = velocity.reshape(3, PZ, NYC, NXC)
    padded_velocity = jnp.concatenate([components[:, :, -1:], components, components[:, :, :1]], axis=2)
    padded_salinity = jnp.concatenate([salinity[:, -1:], salinity, salinity[:, :1]], axis=1)

    def one_block(block):
        start = (block * NYS).astype(jnp.int32)
        coarse_block = lax.dynamic_slice_in_dim(padded_velocity, start, NYS + 2, 2)
        fine_block = lax.dynamic_slice_in_dim(padded_salinity, (start * 3).astype(jnp.int32), 3 * NYS + 2, 1)
        velocity_fine = fine_velocity(coarse_block, wall_index, wall_weight)
        updated = advance(fine_block, velocity_fine, spacing)
        return updated, restrict(updated, wall_index, wall_weight)

    updated, coarse = lax.map(one_block, jnp.arange(N_WN, dtype=jnp.int32))
    salinity_new = jnp.transpose(updated, (1, 0, 2, 3)).reshape(PZF, NYF, NXF)
    coarse_salinity = jnp.transpose(coarse, (1, 0, 2, 3))
    return salinity_new, coarse_salinity
```

```python
import numpy as np
import jax
import jax.numpy as jnp
from jax import lax
from jax.experimental import pallas as pl
from jax.experimental.pallas import tpu as pltpu
from jax.sharding import PartitionSpec as P

TIME_STEP = 0.5
RUNGE_GAMMA = 8.0 / 15.0
DIFFUSIVITY = 0.3

PLANES = 6
ROWS = 12
FINE = 3072
COARSE = 1024
OWNERS = 16
SLAB = 64
BLOCK = 128
BLOCKS = FINE // BLOCK
WINDOW = 256
STACK = 32
HALO_ROWS = 24
CHUNK = 512

f32 = jnp.float32
bf16 = jnp.bfloat16
SCALE = TIME_STEP * RUNGE_GAMMA
FLAT = SCALE * DIFFUSIVITY
SIDE = 0.5 * SCALE / 9.0

ACROSS = [[(1 - plane // 3, 1), (plane // 3, 2)] if plane % 3 == 0 else [(plane // 3, 3)] if plane % 3 == 1 else [(plane // 3, 2), (1 - plane // 3, 1)] for plane in range(PLANES)]
ALONG = [[(row // 3 - 1, 1), (row // 3, 2)] if row % 3 == 0 else [(row // 3, 3)] if row % 3 == 1 else [(row // 3, 2), (row // 3 + 1, 1)] for row in range(ROWS)]


def own_matrix():
    matrix = np.zeros((3, PLANES, 16, STACK), np.float32)
    for c in range(3):
        for plane in range(PLANES):
            for row in range(ROWS):
                for p, a in ACROSS[plane]:
                    for m, b in ALONG[row]:
                        if 0 <= m < 4:
                            matrix[c, plane, row, p * 16 + c * 4 + m] += a * b
    matrix = matrix.reshape(3 * PLANES * 16, STACK)
    return np.concatenate([matrix, matrix], axis=1)


def side_matrix():
    matrix = np.zeros((3, 8, 8), np.float32)
    for c in range(3):
        for plane in range(PLANES):
            for p, a in ACROSS[plane]:
                matrix[c, plane, p * 3 + c] += a
    matrix = matrix.reshape(24, 8)
    return np.concatenate([matrix, matrix], axis=1)


def group_matrices():
    inner = np.zeros((8, PLANES, 16), np.float32)
    outer = np.zeros((8, 8), np.float32)
    for p in range(2):
        for y in range(4):
            inner[p * 4 + y, 3 * p : 3 * p + 3, 3 * y : 3 * y + 3] = 1.0
        inner[:, :, 0] = 0.0
        inner[:, :, ROWS - 1] = 0.0
        outer[p, 3 * p : 3 * p + 3] = 1.0
    return inner.reshape(8, PLANES * 16), outer


OWN_MATRIX = own_matrix()
SIDE_MATRIX = side_matrix()
INNER_GROUPS, OUTER_GROUPS = group_matrices()


def bundle():
    matrix = np.zeros((368, 128), np.float32)
    for first, part in ((0, OWN_MATRIX), (288, INNER_GROUPS), (304, SIDE_MATRIX), (352, OUTER_GROUPS)):
        matrix[first : first + part.shape[0], : part.shape[1]] = part
    return matrix


BUNDLE = bundle()


def window_starts(wall_index):
    starts = []
    for b in range(BLOCKS):
        first = jnp.min(wall_index[b : b + 1, :])
        starts.append(pl.multiple_of(jnp.minimum(lax.shift_right_logical(first, 7) * 128, COARSE - WINDOW), 128))
    return starts


def load_kernel(
    velocity_hbm, salinity_hbm, index_hbm, weight_hbm, spacing_hbm, matrices_hbm,
    send, salinity, index, weight, spacing, matrices, velocity, copied,
):
    copies = [
        pltpu.make_async_copy(source, target, copied.at[number])
        for number, (source, target) in enumerate(
            (
                (velocity_hbm, velocity),
                (salinity_hbm, salinity),
                (index_hbm, index),
                (weight_hbm, weight),
                (spacing_hbm, spacing),
                (matrices_hbm, matrices),
            )
        )
    ]
    for copy in copies:
        copy.start()
    copies[0].wait()
    for q in range(OWNERS):
        for c in range(3):
            for p in range(2):
                send[q, :, c * 128 + p * 64 : c * 128 + p * 64 + 64] = velocity[c, p, q]
    for copy in copies[1:]:
        copy.wait()


def edge_kernel(salinity, arrived, second, first, coarse):
    odd = lax.rem(lax.axis_index("sw"), 2)
    left = lax.broadcasted_iota(jnp.int32, (4, 128), 1) < 64
    for t in range(8):
        lanes = slice(t * 128, t * 128 + 128)
        for c in range(3):
            one = arrived[2 * t, :, c * 128 : c * 128 + 128].astype(f32)
            two = arrived[2 * t + 1, :, c * 128 : c * 128 + 128].astype(f32)
            coarse[c * 4 : c * 4 + 4, lanes] = jnp.where(left, one, pltpu.roll(two, 64, 1))
            coarse[16 + c * 4 : 20 + c * 4, lanes] = jnp.where(left, pltpu.roll(one, 64, 1), two)
    coarse[12:16, :] = jnp.zeros((4, COARSE), f32)
    coarse[28:32, :] = jnp.zeros((4, COARSE), f32)
    for part in range(3):
        lanes = slice(part * 1024, part * 1024 + 1024)
        head = salinity[:, 0, lanes].astype(f32)
        tail = salinity[:, ROWS - 1, lanes].astype(f32)
        second[part * 6 : part * 6 + 6, :] = jnp.where(odd > 0, tail, head).astype(bf16)
        first[part * 6 : part * 6 + 6, :] = jnp.where(odd > 0, head, tail).astype(bf16)
    head = jnp.concatenate([coarse[p * 16 + c * 4 : p * 16 + c * 4 + 1, :] for p in range(2) for c in range(3)], axis=0)
    tail = jnp.concatenate([coarse[p * 16 + c * 4 + 3 : p * 16 + c * 4 + 4, :] for p in range(2) for c in range(3)], axis=0)
    second[18:24, :] = jnp.where(odd > 0, tail, head).astype(bf16)
    first[18:24, :] = jnp.where(odd > 0, head, tail).astype(bf16)


def inner_kernel(
    salinity, coarse, wall_index, wall_weight, spacing, matrices,
    updated, edges, grouped, hits, turned_hits, field, factors, sources, normal,
):
    width = spacing[...]
    before = pltpu.roll(width, 1, 1)
    after = pltpu.roll(width, FINE - 1, 1)
    column = lax.broadcasted_iota(jnp.int32, (1, FINE), 1)
    gap_low = jnp.where(column == 0, width, 0.5 * (before + width))
    gap_high = jnp.where(column == FINE - 1, width, 0.5 * (width + after))
    factors[0:1, :] = FLAT / (gap_high * width)
    factors[1:2, :] = FLAT / (gap_low * width)
    factors[2:3, :] = (SCALE / 9.0) / (gap_low + gap_high)

    for plane in range(PLANES):
        field[plane, 0:ROWS, :] = salinity[plane].astype(f32)
        field[plane, ROWS:16, :] = jnp.zeros((16 - ROWS, FINE), f32)

    starts = window_starts(wall_index)
    whole = coarse[...]
    sources[0:STACK, :] = whole.astype(bf16)
    sources[STACK : 2 * STACK, :] = pltpu.roll(whole, COARSE - 1, 1).astype(bf16)
    table = jnp.concatenate([wall_index[...].astype(f32), jnp.zeros((128 - BLOCKS, BLOCK), f32)], axis=0)
    columns = table.T.astype(jnp.int32)
    cell = lax.broadcasted_iota(jnp.int32, (WINDOW, BLOCK), 0)
    turned_cell = lax.broadcasted_iota(jnp.int32, (BLOCK, WINDOW), 1)
    for b in range(BLOCKS):
        lanes = slice(b * BLOCK, b * BLOCK + BLOCK)
        hit = jnp.where(cell == wall_index[b : b + 1, :] - starts[b], 1.0, 0.0).astype(bf16)
        hits[b] = hit
        turned_hits[b] = jnp.where(turned_cell == columns[:, b : b + 1] - starts[b], 1.0, 0.0).astype(bf16)
        both = jnp.dot(sources[:, pl.ds(starts[b], WINDOW)], hit, preferred_element_type=f32)
        weight = wall_weight[:, lanes]
        value = (1.0 - weight) * both[0:STACK] + weight * both[STACK : 2 * STACK]
        upper = value.astype(bf16)
        normal[0:STACK, lanes] = upper
        normal[STACK : 2 * STACK, lanes] = (value - upper.astype(f32)).astype(bf16)

    lane = lax.broadcasted_iota(jnp.int32, (16, BLOCK), 1)
    for b in range(BLOCKS):
        lanes = slice(b * BLOCK, b * BLOCK + BLOCK)
        velocity = jnp.dot(matrices[0:288, 0:64], normal[:, lanes], preferred_element_type=f32)
        up = factors[0:1, lanes]
        down = factors[1:2, lanes]
        slant = factors[2:3, lanes]
        block = [field[plane, :, lanes] for plane in range(PLANES)]
        results = []
        for plane in range(PLANES):
            here = block[plane]
            if b == 0:
                low_side = -here[:, 0:1]
            else:
                low_side = pltpu.roll(field[plane, :, (b - 1) * BLOCK : b * BLOCK], 1, 1)
            if b == BLOCKS - 1:
                high_side = -here[:, BLOCK - 1 : BLOCK]
            else:
                high_side = pltpu.roll(field[plane, :, (b + 1) * BLOCK : (b + 2) * BLOCK], BLOCK - 1, 1)
            wall_low = jnp.where(lane == 0, low_side, pltpu.roll(here, 1, 1))
            wall_high = jnp.where(lane == BLOCK - 1, high_side, pltpu.roll(here, BLOCK - 1, 1))
            forward = pltpu.roll(here, 15, 0)
            behind = pltpu.roll(here, 1, 0)
            span_low = block[(plane - 1) % PLANES]
            span_high = block[(plane + 1) % PLANES]
            u = velocity[plane * 16 : plane * 16 + 16]
            v = velocity[96 + plane * 16 : 96 + plane * 16 + 16]
            w = velocity[192 + plane * 16 : 192 + plane * 16 + 16]
            along = SIDE * (forward - behind)
            slope = (wall_high - wall_low) * slant
            across = SIDE * (span_high - span_low)
            new = here + (wall_high - here) * up - (here - wall_low) * down
            new = new + FLAT * ((forward + behind) + (span_high + span_low) - 4.0 * here)
            new = new - (u * along + v * slope + w * across)
            for number, value in enumerate((new, u, along, slope, across)):
                edges[number, plane : plane + 1, lanes] = value[0:1]
                edges[number, 8 + plane : 9 + plane, lanes] = value[ROWS - 1 : ROWS]
            new = new.astype(bf16)
            updated[plane, :, lanes] = new[0:ROWS]
            results.append(new)
        stacked = jnp.concatenate(results, axis=0)
        grouped[:, lanes] = jnp.dot(matrices[288:296, 0:96], stacked, preferred_element_type=f32)


def edge_row(message, base, sign, edges, hits, starts, wall_weight, matrices, sources, raw, normal):
    column = message[18:24, :].astype(f32)
    spare = jnp.zeros((2, COARSE), f32)
    column = jnp.concatenate([column, spare], axis=0)
    sources[0:16, :] = jnp.concatenate([column, pltpu.roll(column, COARSE - 1, 1)], axis=0).astype(bf16)
    for b in range(BLOCKS):
        lanes = slice(b * BLOCK, b * BLOCK + BLOCK)
        raw[:, lanes] = jnp.dot(sources[:, pl.ds(starts[b], WINDOW)], hits[b], preferred_element_type=f32)
    results = []
    spare = jnp.zeros((2, CHUNK), f32)
    for k in range(FINE // CHUNK):
        lanes = slice(k * CHUNK, k * CHUNK + CHUNK)
        weight = wall_weight[:, lanes]
        value = (1.0 - weight) * raw[0:8, lanes] + weight * raw[8:16, lanes]
        upper = value.astype(bf16).astype(f32)
        normal[:, lanes] = jnp.concatenate([upper, value - upper], axis=0).astype(bf16)
        velocity = jnp.dot(matrices[304:328, 0:16], normal[:, lanes], preferred_element_type=f32)
        part, offset = divmod(k * CHUNK, 1024)
        ghost = message[part * 6 : part * 6 + 6, offset : offset + CHUNK].astype(f32)
        ghost = jnp.concatenate([ghost, spare], axis=0)
        pull = sign * ghost
        at = pl.ds(base, 8)
        new = edges[0, at, lanes] + FLAT * ghost + edges[1, at, lanes] * pull
        new = new + velocity[0:8] * (pull - edges[2, at, lanes])
        new = new - velocity[8:16] * edges[3, at, lanes] - velocity[16:24] * edges[4, at, lanes]
        results.append(new.astype(bf16))
    return results


def split_terms(sums, weight):
    sums = sums * (1.0 / 9.0)
    above = sums * weight
    below = sums - above
    below_upper = below.astype(bf16).astype(f32)
    above_upper = above.astype(bf16).astype(f32)
    return jnp.concatenate([below_upper, below - below_upper, above_upper, above - above_upper], axis=0).astype(bf16)


def near_kernel(
    message, inner, edges, grouped, hits, turned_hits, wall_index, wall_weight, matrices,
    updated, sums, total, sources, raw, normal, terms, parts,
):
    odd = lax.rem(lax.axis_index("sw"), 2)
    starts = window_starts(wall_index)
    base = pl.multiple_of(8 * (1 - odd), 8)
    sign = jnp.where(odd > 0, SIDE, -SIDE)
    edge = jnp.where(odd > 0, 0, ROWS - 1)
    rows = edge_row(message, base, sign, edges, hits, starts, wall_weight, matrices, sources, raw, normal)
    own = lax.broadcasted_iota(jnp.int32, (8, CHUNK), 0)
    far = jnp.where(odd > 0, 3, 0)
    row = lax.broadcasted_iota(jnp.int32, (ROWS, CHUNK), 0)
    for k, rounded in enumerate(rows):
        lanes = slice(k * CHUNK, k * CHUNK + CHUNK)
        added = jnp.dot(matrices[352:360, 0:8], rounded, preferred_element_type=f32)
        near = 3 - far
        low = jnp.where(own == near, added[0:1], jnp.where(own == near + 4, added[1:2], 0.0))
        whole = grouped[:, lanes] + low
        waiting = jnp.logical_or(own == far, own == far + 4)
        late = jnp.where(waiting, whole, 0.0)
        sums[:, lanes] = jnp.concatenate(
            [jnp.sum(late[0:4], axis=0, keepdims=True), jnp.sum(late[4:8], axis=0, keepdims=True), jnp.zeros((6, CHUNK), f32)],
            axis=0,
        )
        terms[:, lanes] = split_terms(whole - late, wall_weight[:, lanes])
        new = rounded.astype(f32)
        for plane in range(PLANES):
            kept = jnp.where(row == edge, new[plane : plane + 1], inner[plane, :, lanes].astype(f32))
            updated[plane, :, lanes] = kept.astype(bf16)
    for b in range(BLOCKS):
        lanes = slice(b * BLOCK, b * BLOCK + BLOCK)
        parts[b] = jnp.dot(terms[:, lanes], turned_hits[b], preferred_element_type=f32)
    total[...] = jnp.zeros_like(total)
    for b in range(BLOCKS):
        part = parts[b]
        total[0:8, pl.ds(starts[b], WINDOW)] += part[0:8] + part[8:16]
        total[8:16, pl.ds(starts[b], WINDOW)] += part[16:24] + part[24:32]


def far_kernel(
    message, near, sums, near_total, edges, hits, turned_hits, wall_index, wall_weight, matrices,
    updated_hbm, send, sources, raw, normal, terms, parts, total, updated, copied,
):
    odd = lax.rem(lax.axis_index("sw"), 2)
    starts = window_starts(wall_index)
    base = pl.multiple_of(8 * odd, 8)
    sign = jnp.where(odd > 0, -SIDE, SIDE)
    edge = jnp.where(odd > 0, ROWS - 1, 0)
    rows = edge_row(message, base, sign, edges, hits, starts, wall_weight, matrices, sources, raw, normal)
    chunks = [slice(k * CHUNK, k * CHUNK + CHUNK) for k in range(FINE // CHUNK)]
    row = lax.broadcasted_iota(jnp.int32, (ROWS, CHUNK), 0)
    copies = []
    for plane in range(PLANES):
        for lanes, rounded in zip(chunks, rows):
            new = rounded[plane : plane + 1].astype(f32)
            updated[plane, :, lanes] = jnp.where(row == edge, new, near[plane, :, lanes].astype(f32)).astype(bf16)
        copy = pltpu.make_async_copy(updated.at[plane], updated_hbm.at[plane], copied.at[plane])
        copy.start()
        copies.append(copy)

    spare = jnp.zeros((8, CHUNK), bf16)
    for lanes, rounded in zip(chunks, rows):
        whole = sums[:, lanes] + jnp.dot(matrices[352:360, 0:8], rounded, preferred_element_type=f32)
        terms[:, lanes] = jnp.concatenate([split_terms(whole[0:2], wall_weight[:, lanes]), spare], axis=0)
    for b in range(BLOCKS):
        lanes = slice(b * BLOCK, b * BLOCK + BLOCK)
        parts[b] = jnp.dot(terms[:, lanes], turned_hits[b], preferred_element_type=f32)[0:8]

    total[...] = jnp.zeros_like(total)
    for b in range(BLOCKS):
        total[:, pl.ds(starts[b], WINDOW)] += parts[b]
    last = lax.broadcasted_iota(jnp.int32, (8, COARSE), 1)
    own = lax.broadcasted_iota(jnp.int32, (8, COARSE), 0)
    far = jnp.where(odd > 0, 3, 0)
    below = total[0:2] + total[2:4]
    above = total[4:6] + total[6:8]
    below = jnp.where(own == far, below[0:1], jnp.where(own == far + 4, below[1:2], near_total[0:8, :]))
    above = jnp.where(own == far, above[0:1], jnp.where(own == far + 4, above[1:2], near_total[8:16, :]))
    restricted = below + jnp.where(last == 0, 0.0, pltpu.roll(above, 1, 1))
    left = lax.broadcasted_iota(jnp.int32, (4, 128), 1) < 64
    for t in range(8):
        tile = restricted[:, t * 128 : t * 128 + 128]
        turned = pltpu.roll(tile, 64, 1)
        send[2 * t] = jnp.where(left, tile[0:4], turned[4:8]).astype(bf16)
        send[2 * t + 1] = jnp.where(left, turned[0:4], tile[4:8]).astype(bf16)
    for copy in copies:
        copy.wait()


def spread_kernel(arrived, coarse):
    for q in range(OWNERS):
        for p in range(2):
            coarse[p, q] = arrived[q, :, p * 64 : p * 64 + 64]


VMEM = pl.BlockSpec(memory_space=pltpu.VMEM)
ANY = pl.BlockSpec(memory_space=pl.ANY)


def call(kernel, shapes, in_specs, scratch=(), megabytes=16, cost=None, out_specs=None):
    single = not isinstance(shapes, list)
    return pl.pallas_call(
        kernel,
        out_shape=shapes,
        in_specs=in_specs,
        out_specs=out_specs or (VMEM if single else [VMEM] * len(shapes)),
        scratch_shapes=list(scratch),
        cost_estimate=cost,
        compiler_params=pltpu.CompilerParams(vmem_limit_bytes=megabytes * 1024 * 1024),
    )


def body(salinity, velocity, wall_index, wall_weight, spacing):
    total_count = lax.axis_size("sw") * lax.axis_size("wn")
    near = [(i, i ^ 1) for i in range(total_count)]
    far = []
    for i in range(total_count):
        far.append((i, (i + 1) % total_count if i % 2 else (i - 1) % total_count))

    matrices = jnp.asarray(BUNDLE, bf16)
    message = jax.ShapeDtypeStruct((HALO_ROWS, COARSE), bf16)
    fine = jax.ShapeDtypeStruct((PLANES, ROWS, FINE), bf16)
    own, salinity, wall_index, wall_weight, spacing, matrices = call(
        load_kernel,
        [
            pltpu.VMEM((OWNERS, 4, 384), bf16),
            pltpu.VMEM((PLANES, ROWS, FINE), bf16),
            pltpu.VMEM((BLOCKS, BLOCK), jnp.int32),
            pltpu.VMEM((1, FINE), f32),
            pltpu.VMEM((1, FINE), f32),
            pltpu.VMEM((368, 128), bf16),
        ],
        [ANY] * 6,
        [pltpu.VMEM((3, 2, OWNERS, 4, SLAB), bf16), pltpu.SemaphoreType.DMA((6,))],
        megabytes=56,
    )(velocity, salinity, wall_index.reshape(BLOCKS, BLOCK), wall_weight[None], spacing[None], matrices)
    arrived = lax.all_to_all(own, "wn", split_axis=0, concat_axis=0, tiled=True)
    second, first, coarse = call(
        edge_kernel, [message, message, jax.ShapeDtypeStruct((STACK, COARSE), f32)], [VMEM] * 2
    )(salinity, arrived)
    second_in = lax.ppermute(second, ("wn", "sw"), far)
    first_in = lax.ppermute(first, ("wn", "sw"), near)
    inner = call(
        inner_kernel,
        [
            fine,
            jax.ShapeDtypeStruct((5, 16, FINE), f32),
            jax.ShapeDtypeStruct((8, FINE), f32),
            jax.ShapeDtypeStruct((BLOCKS, WINDOW, BLOCK), bf16),
            jax.ShapeDtypeStruct((BLOCKS, BLOCK, WINDOW), bf16),
        ],
        [VMEM] * 6,
        [
            pltpu.VMEM((PLANES, 16, FINE), f32),
            pltpu.VMEM((8, FINE), f32),
            pltpu.VMEM((2 * STACK, COARSE), bf16),
            pltpu.VMEM((2 * STACK, FINE), bf16),
        ],
        cost=pl.CostEstimate(flops=4_000_000_000, bytes_accessed=2_000_000_000, transcendentals=0),
    )(
        salinity, coarse, wall_index, wall_weight, spacing, matrices,
    )
    interior, edges, grouped, hits, turned_hits = inner
    work = [
        pltpu.VMEM((16, COARSE), bf16),
        pltpu.VMEM((16, FINE), f32),
        pltpu.VMEM((16, FINE), bf16),
    ]
    near_updated, sums, near_total = call(
        near_kernel,
        [fine, jax.ShapeDtypeStruct((8, FINE), f32), jax.ShapeDtypeStruct((16, COARSE), f32)],
        [VMEM] * 9,
        work + [pltpu.VMEM((32, FINE), bf16), pltpu.VMEM((BLOCKS, 32, WINDOW), f32)],
        cost=pl.CostEstimate(flops=1000, bytes_accessed=1000, transcendentals=0),
    )(first_in, interior, edges, grouped, hits, turned_hits, wall_index, wall_weight, matrices)
    updated, send = call(
        far_kernel,
        [fine, jax.ShapeDtypeStruct((OWNERS, 4, 128), bf16)],
        [VMEM] * 10,
        work
        + [
            pltpu.VMEM((16, FINE), bf16),
            pltpu.VMEM((BLOCKS, 8, WINDOW), f32),
            pltpu.VMEM((8, COARSE), f32),
            pltpu.VMEM((PLANES, ROWS, FINE), bf16),
            pltpu.SemaphoreType.DMA((PLANES,)),
        ],
        out_specs=[ANY, VMEM],
    )(second_in, near_updated, sums, near_total, edges, hits, turned_hits, wall_index, wall_weight, matrices)
    back = lax.all_to_all(send, "wn", split_axis=0, concat_axis=0, tiled=True)
    coarse = call(spread_kernel, jax.ShapeDtypeStruct((2, OWNERS, 4, SLAB), bf16), [VMEM])(back)
    return (updated, coarse)


def solution(mesh):
    in_specs = (P(None, ("wn", "sw"), None), P(None, None, None, "sw", "wn"), P(), P(), P())
    out_specs = (P(None, ("wn", "sw"), None), P(None, None, "sw", "wn"))
    return jax.shard_map(body, mesh=mesh, in_specs=in_specs, out_specs=out_specs, check_vma=False)
```

```python
import numpy as np
import jax
import jax.numpy as jnp
from jax import lax
from jax.experimental import pallas as pl
from jax.experimental.pallas import tpu as pltpu
from jax.sharding import PartitionSpec as P

TIME_STEP = 0.5
RUNGE_GAMMA = 8.0 / 15.0
DIFFUSIVITY = 0.3

PLANES = 6
ROWS = 12
FINE = 3072
COARSE = 1024
OWNERS = 16
SLAB = 64
BLOCK = 128
BLOCKS = FINE // BLOCK
ORDER = [6, 7, 8, 9, 10, 11, 12, 13, 14, 15, 0, 1, 2, 3, 4, 5]
SLOT = [ORDER.index(q) for q in range(16)]
WINDOW = 256
STACK = 32
HALO_ROWS = 24
CHUNK = 512

f32 = jnp.float32
bf16 = jnp.bfloat16
SCALE = TIME_STEP * RUNGE_GAMMA
FLAT = SCALE * DIFFUSIVITY
SIDE = 0.5 * SCALE / 9.0

ACROSS = [[(1 - plane // 3, 1), (plane // 3, 2)] if plane % 3 == 0 else [(plane // 3, 3)] if plane % 3 == 1 else [(plane // 3, 2), (1 - plane // 3, 1)] for plane in range(PLANES)]
ALONG = [[(row // 3 - 1, 1), (row // 3, 2)] if row % 3 == 0 else [(row // 3, 3)] if row % 3 == 1 else [(row // 3, 2), (row // 3 + 1, 1)] for row in range(ROWS)]


def own_matrix():
    matrix = np.zeros((3, PLANES, 16, STACK), np.float32)
    for c in range(3):
        for plane in range(PLANES):
            for row in range(ROWS):
                for p, a in ACROSS[plane]:
                    for m, b in ALONG[row]:
                        if 0 <= m < 4:
                            matrix[c, plane, row, p * 16 + c * 4 + m] += a * b
    matrix = matrix.reshape(3 * PLANES * 16, STACK)
    return np.concatenate([matrix, matrix], axis=1)


def side_matrix():
    matrix = np.zeros((3, 8, 8), np.float32)
    for c in range(3):
        for plane in range(PLANES):
            for p, a in ACROSS[plane]:
                matrix[c, plane, p * 3 + c] += a
    matrix = matrix.reshape(24, 8)
    return np.concatenate([matrix, matrix], axis=1)


def group_matrices():
    inner = np.zeros((8, PLANES, 16), np.float32)
    outer = np.zeros((8, 8), np.float32)
    for p in range(2):
        for y in range(4):
            inner[p * 4 + y, 3 * p : 3 * p + 3, 3 * y : 3 * y + 3] = 1.0
        inner[:, :, 0] = 0.0
        inner[:, :, ROWS - 1] = 0.0
        outer[p, 3 * p : 3 * p + 3] = 1.0
    return inner.reshape(8, PLANES * 16), outer


OWN_MATRIX = own_matrix()
SIDE_MATRIX = side_matrix()
INNER_GROUPS, OUTER_GROUPS = group_matrices()


def bundle():
    matrix = np.zeros((368, 128), np.float32)
    for first, part in ((0, OWN_MATRIX), (288, INNER_GROUPS), (304, SIDE_MATRIX), (352, OUTER_GROUPS)):
        matrix[first : first + part.shape[0], : part.shape[1]] = part
    return matrix


BUNDLE = bundle()


def window_starts(wall_index):
    starts = []
    for b in range(BLOCKS):
        first = jnp.min(wall_index[b : b + 1, :])
        starts.append(pl.multiple_of(jnp.minimum(lax.shift_right_logical(first, 7) * 128, COARSE - WINDOW), 128))
    return starts


def load_kernel(
    velocity_hbm, salinity_hbm, index_hbm, weight_hbm, spacing_hbm, matrices_hbm,
    send, salinity, index, weight, spacing, matrices, velocity, copied,
):
    copies = [
        pltpu.make_async_copy(source, target, copied.at[number])
        for number, (source, target) in enumerate(
            (
                (velocity_hbm, velocity),
                (salinity_hbm, salinity),
                (index_hbm, index),
                (weight_hbm, weight),
                (spacing_hbm, spacing),
                (matrices_hbm, matrices),
            )
        )
    ]
    for copy in copies:
        copy.start()
    copies[0].wait()
    for q in range(OWNERS):
        for c in range(3):
            for p in range(2):
                send[SLOT[q], :, c * 128 + p * 64 : c * 128 + p * 64 + 64] = velocity[c, p, q]
    for copy in copies[1:]:
        copy.wait()


def edge_kernel(salinity, arrived, second, first, coarse):
    odd = lax.rem(lax.axis_index("sw"), 2)
    left = lax.broadcasted_iota(jnp.int32, (4, 128), 1) < 64
    for t in range(8):
        lanes = slice(t * 128, t * 128 + 128)
        for c in range(3):
            one = arrived[SLOT[2 * t], :, c * 128 : c * 128 + 128].astype(f32)
            two = arrived[SLOT[2 * t + 1], :, c * 128 : c * 128 + 128].astype(f32)
            coarse[c * 4 : c * 4 + 4, lanes] = jnp.where(left, one, pltpu.roll(two, 64, 1))
            coarse[16 + c * 4 : 20 + c * 4, lanes] = jnp.where(left, pltpu.roll(one, 64, 1), two)
    coarse[12:16, :] = jnp.zeros((4, COARSE), f32)
    coarse[28:32, :] = jnp.zeros((4, COARSE), f32)
    for part in range(3):
        lanes = slice(part * 1024, part * 1024 + 1024)
        head = salinity[:, 0, lanes].astype(f32)
        tail = salinity[:, ROWS - 1, lanes].astype(f32)
        second[part * 6 : part * 6 + 6, :] = jnp.where(odd > 0, tail, head).astype(bf16)
        first[part * 6 : part * 6 + 6, :] = jnp.where(odd > 0, head, tail).astype(bf16)
    head = jnp.concatenate([coarse[p * 16 + c * 4 : p * 16 + c * 4 + 1, :] for p in range(2) for c in range(3)], axis=0)
    tail = jnp.concatenate([coarse[p * 16 + c * 4 + 3 : p * 16 + c * 4 + 4, :] for p in range(2) for c in range(3)], axis=0)
    second[18:24, :] = jnp.where(odd > 0, tail, head).astype(bf16)
    first[18:24, :] = jnp.where(odd > 0, head, tail).astype(bf16)


def inner_kernel(
    salinity, coarse, wall_index, wall_weight, spacing, matrices,
    updated, edges, grouped, hits, turned_hits, field, factors, sources, normal,
):
    width = spacing[...]
    before = pltpu.roll(width, 1, 1)
    after = pltpu.roll(width, FINE - 1, 1)
    column = lax.broadcasted_iota(jnp.int32, (1, FINE), 1)
    gap_low = jnp.where(column == 0, width, 0.5 * (before + width))
    gap_high = jnp.where(column == FINE - 1, width, 0.5 * (width + after))
    factors[0:1, :] = FLAT / (gap_high * width)
    factors[1:2, :] = FLAT / (gap_low * width)
    factors[2:3, :] = (SCALE / 9.0) / (gap_low + gap_high)

    for plane in range(PLANES):
        field[plane, 0:ROWS, :] = salinity[plane].astype(f32)
        field[plane, ROWS:16, :] = jnp.zeros((16 - ROWS, FINE), f32)

    starts = window_starts(wall_index)
    whole = coarse[...]
    sources[0:STACK, :] = whole.astype(bf16)
    sources[STACK : 2 * STACK, :] = pltpu.roll(whole, COARSE - 1, 1).astype(bf16)
    table = jnp.concatenate([wall_index[...].astype(f32), jnp.zeros((128 - BLOCKS, BLOCK), f32)], axis=0)
    columns = table.T.astype(jnp.int32)
    cell = lax.broadcasted_iota(jnp.int32, (WINDOW, BLOCK), 0)
    turned_cell = lax.broadcasted_iota(jnp.int32, (BLOCK, WINDOW), 1)
    for b in range(BLOCKS):
        lanes = slice(b * BLOCK, b * BLOCK + BLOCK)
        hit = jnp.where(cell == wall_index[b : b + 1, :] - starts[b], 1.0, 0.0).astype(bf16)
        hits[b] = hit
        turned_hits[b] = jnp.where(turned_cell == columns[:, b : b + 1] - starts[b], 1.0, 0.0).astype(bf16)
        both = jnp.dot(sources[:, pl.ds(starts[b], WINDOW)], hit, preferred_element_type=f32)
        weight = wall_weight[:, lanes]
        value = (1.0 - weight) * both[0:STACK] + weight * both[STACK : 2 * STACK]
        upper = value.astype(bf16)
        normal[0:STACK, lanes] = upper
        normal[STACK : 2 * STACK, lanes] = (value - upper.astype(f32)).astype(bf16)

    lane = lax.broadcasted_iota(jnp.int32, (16, BLOCK), 1)
    for b in range(BLOCKS):
        lanes = slice(b * BLOCK, b * BLOCK + BLOCK)
        velocity = jnp.dot(matrices[0:288, 0:64], normal[:, lanes], preferred_element_type=f32)
        up = factors[0:1, lanes]
        down = factors[1:2, lanes]
        slant = factors[2:3, lanes]
        block = [field[plane, :, lanes] for plane in range(PLANES)]
        results = []
        for plane in range(PLANES):
            here = block[plane]
            if b == 0:
                low_side = -here[:, 0:1]
            else:
                low_side = pltpu.roll(field[plane, :, (b - 1) * BLOCK : b * BLOCK], 1, 1)
            if b == BLOCKS - 1:
                high_side = -here[:, BLOCK - 1 : BLOCK]
            else:
                high_side = pltpu.roll(field[plane, :, (b + 1) * BLOCK : (b + 2) * BLOCK], BLOCK - 1, 1)
            wall_low = jnp.where(lane == 0, low_side, pltpu.roll(here, 1, 1))
            wall_high = jnp.where(lane == BLOCK - 1, high_side, pltpu.roll(here, BLOCK - 1, 1))
            forward = pltpu.roll(here, 15, 0)
            behind = pltpu.roll(here, 1, 0)
            span_low = block[(plane - 1) % PLANES]
            span_high = block[(plane + 1) % PLANES]
            u = velocity[plane * 16 : plane * 16 + 16]
            v = velocity[96 + plane * 16 : 96 + plane * 16 + 16]
            w = velocity[192 + plane * 16 : 192 + plane * 16 + 16]
            along = SIDE * (forward - behind)
            slope = (wall_high - wall_low) * slant
            across = SIDE * (span_high - span_low)
            new = here + (wall_high - here) * up - (here - wall_low) * down
            new = new + FLAT * ((forward + behind) + (span_high + span_low) - 4.0 * here)
            new = new - (u * along + v * slope + w * across)
            for number, value in enumerate((new, u, along, slope, across)):
                edges[number, plane : plane + 1, lanes] = value[0:1]
                edges[number, 8 + plane : 9 + plane, lanes] = value[ROWS - 1 : ROWS]
            new = new.astype(bf16)
            updated[plane, :, lanes] = new[0:ROWS]
            results.append(new)
        stacked = jnp.concatenate(results, axis=0)
        grouped[:, lanes] = jnp.dot(matrices[288:296, 0:96], stacked, preferred_element_type=f32)


def edge_row(message, base, sign, edges, hits, starts, wall_weight, matrices, sources, raw, normal):
    column = message[18:24, :].astype(f32)
    spare = jnp.zeros((2, COARSE), f32)
    column = jnp.concatenate([column, spare], axis=0)
    sources[0:16, :] = jnp.concatenate([column, pltpu.roll(column, COARSE - 1, 1)], axis=0).astype(bf16)
    for b in range(BLOCKS):
        lanes = slice(b * BLOCK, b * BLOCK + BLOCK)
        raw[:, lanes] = jnp.dot(sources[:, pl.ds(starts[b], WINDOW)], hits[b], preferred_element_type=f32)
    results = []
    spare = jnp.zeros((2, CHUNK), f32)
    planes = lax.broadcasted_iota(jnp.int32, (8, CHUNK), 0)
    for k in range(FINE // CHUNK):
        lanes = slice(k * CHUNK, k * CHUNK + CHUNK)
        weight = wall_weight[:, lanes]
        value = (1.0 - weight) * raw[0:8, lanes] + weight * raw[8:16, lanes]
        upper = value.astype(bf16).astype(f32)
        normal[:, lanes] = jnp.concatenate([upper, value - upper], axis=0).astype(bf16)
        velocity = jnp.dot(matrices[304:328, 0:16], normal[:, lanes], preferred_element_type=f32)
        part, offset = divmod(k * CHUNK, 1024)
        ghost = message[part * 6 : part * 6 + 6, offset : offset + CHUNK].astype(f32)
        ghost = jnp.concatenate([ghost, spare], axis=0)
        pull = sign * ghost
        at = pl.ds(base, 8)
        new = edges[0, at, lanes] + FLAT * ghost + edges[1, at, lanes] * pull
        new = new + velocity[0:8] * (pull - edges[2, at, lanes])
        new = new - velocity[8:16] * edges[3, at, lanes] - velocity[16:24] * edges[4, at, lanes]
        results.append(jnp.where(planes < PLANES, new, 0.0).astype(bf16))
    return results


def split_terms(sums, weight):
    sums = sums * (1.0 / 9.0)
    above = sums * weight
    below = sums - above
    below_upper = below.astype(bf16).astype(f32)
    above_upper = above.astype(bf16).astype(f32)
    return jnp.concatenate([below_upper, below - below_upper, above_upper, above - above_upper], axis=0).astype(bf16)


def near_kernel(
    message, inner, edges, grouped, hits, turned_hits, wall_index, wall_weight, matrices,
    updated, sums, total, sources, raw, normal, terms, parts,
):
    odd = lax.rem(lax.axis_index("sw"), 2)
    starts = window_starts(wall_index)
    base = pl.multiple_of(8 * (1 - odd), 8)
    sign = jnp.where(odd > 0, SIDE, -SIDE)
    edge = jnp.where(odd > 0, 0, ROWS - 1)
    rows = edge_row(message, base, sign, edges, hits, starts, wall_weight, matrices, sources, raw, normal)
    own = lax.broadcasted_iota(jnp.int32, (8, CHUNK), 0)
    far = jnp.where(odd > 0, 3, 0)
    row = lax.broadcasted_iota(jnp.int32, (ROWS, CHUNK), 0)
    for k, rounded in enumerate(rows):
        lanes = slice(k * CHUNK, k * CHUNK + CHUNK)
        added = jnp.dot(matrices[352:360, 0:8], rounded, preferred_element_type=f32)
        near = 3 - far
        low = jnp.where(own == near, added[0:1], jnp.where(own == near + 4, added[1:2], 0.0))
        whole = grouped[:, lanes] + low
        waiting = jnp.logical_or(own == far, own == far + 4)
        late = jnp.where(waiting, whole, 0.0)
        sums[:, lanes] = jnp.concatenate(
            [jnp.sum(late[0:4], axis=0, keepdims=True), jnp.sum(late[4:8], axis=0, keepdims=True), jnp.zeros((6, CHUNK), f32)],
            axis=0,
        )
        terms[:, lanes] = split_terms(whole - late, wall_weight[:, lanes])
        new = rounded.astype(f32)
        for plane in range(PLANES):
            kept = jnp.where(row == edge, new[plane : plane + 1], inner[plane, :, lanes].astype(f32))
            updated[plane, :, lanes] = kept.astype(bf16)
    for b in range(BLOCKS):
        lanes = slice(b * BLOCK, b * BLOCK + BLOCK)
        parts[b] = jnp.dot(terms[:, lanes], turned_hits[b], preferred_element_type=f32)
    total[...] = jnp.zeros_like(total)
    for b in range(BLOCKS):
        part = parts[b]
        total[0:8, pl.ds(starts[b], WINDOW)] += part[0:8] + part[8:16]
        total[8:16, pl.ds(starts[b], WINDOW)] += part[16:24] + part[24:32]


def far_kernel(
    message, near, sums, near_total, edges, hits, turned_hits, wall_index, wall_weight, matrices,
    updated_hbm, send, sources, raw, normal, terms, parts, total, updated, copied,
):
    odd = lax.rem(lax.axis_index("sw"), 2)
    starts = window_starts(wall_index)
    base = pl.multiple_of(8 * odd, 8)
    sign = jnp.where(odd > 0, -SIDE, SIDE)
    edge = jnp.where(odd > 0, ROWS - 1, 0)
    rows = edge_row(message, base, sign, edges, hits, starts, wall_weight, matrices, sources, raw, normal)
    chunks = [slice(k * CHUNK, k * CHUNK + CHUNK) for k in range(FINE // CHUNK)]
    row = lax.broadcasted_iota(jnp.int32, (ROWS, CHUNK), 0)
    copies = []
    for plane in range(PLANES):
        for lanes, rounded in zip(chunks, rows):
            new = rounded[plane : plane + 1].astype(f32)
            updated[plane, :, lanes] = jnp.where(row == edge, new, near[plane, :, lanes].astype(f32)).astype(bf16)
        copy = pltpu.make_async_copy(updated.at[plane], updated_hbm.at[plane], copied.at[plane])
        copy.start()
        copies.append(copy)

    spare = jnp.zeros((8, CHUNK), bf16)
    for lanes, rounded in zip(chunks, rows):
        whole = sums[:, lanes] + jnp.dot(matrices[352:360, 0:8], rounded, preferred_element_type=f32)
        terms[:, lanes] = jnp.concatenate([split_terms(whole[0:2], wall_weight[:, lanes]), spare], axis=0)
    for b in range(BLOCKS):
        lanes = slice(b * BLOCK, b * BLOCK + BLOCK)
        parts[b] = jnp.dot(terms[:, lanes], turned_hits[b], preferred_element_type=f32)[0:8]

    total[...] = jnp.zeros_like(total)
    for b in range(BLOCKS):
        total[:, pl.ds(starts[b], WINDOW)] += parts[b]
    last = lax.broadcasted_iota(jnp.int32, (8, COARSE), 1)
    own = lax.broadcasted_iota(jnp.int32, (8, COARSE), 0)
    far = jnp.where(odd > 0, 3, 0)
    below = total[0:2] + total[2:4]
    above = total[4:6] + total[6:8]
    below = jnp.where(own == far, below[0:1], jnp.where(own == far + 4, below[1:2], near_total[0:8, :]))
    above = jnp.where(own == far, above[0:1], jnp.where(own == far + 4, above[1:2], near_total[8:16, :]))
    restricted = below + jnp.where(last == 0, 0.0, pltpu.roll(above, 1, 1))
    left = lax.broadcasted_iota(jnp.int32, (4, 128), 1) < 64
    for t in range(8):
        tile = restricted[:, t * 128 : t * 128 + 128]
        turned = pltpu.roll(tile, 64, 1)
        send[SLOT[2 * t]] = jnp.where(left, tile[0:4], turned[4:8]).astype(bf16)
        send[SLOT[2 * t + 1]] = jnp.where(left, turned[0:4], tile[4:8]).astype(bf16)
    for copy in copies:
        copy.wait()


def spread_kernel(arrived, coarse):
    for q in range(OWNERS):
        for p in range(2):
            coarse[p, q] = arrived[SLOT[q], :, p * 64 : p * 64 + 64]


VMEM = pl.BlockSpec(memory_space=pltpu.VMEM)
ANY = pl.BlockSpec(memory_space=pl.ANY)


def call(kernel, shapes, in_specs, scratch=(), megabytes=16, cost=None, out_specs=None):
    single = not isinstance(shapes, list)
    return pl.pallas_call(
        kernel,
        out_shape=shapes,
        in_specs=in_specs,
        out_specs=out_specs or (VMEM if single else [VMEM] * len(shapes)),
        scratch_shapes=list(scratch),
        cost_estimate=cost,
        compiler_params=pltpu.CompilerParams(vmem_limit_bytes=megabytes * 1024 * 1024),
    )


def body(salinity, velocity, wall_index, wall_weight, spacing):
    total_count = lax.axis_size("sw") * lax.axis_size("wn")
    near = [(i, i ^ 1) for i in range(total_count)]
    far = []
    for i in range(total_count):
        far.append((i, (i + 1) % total_count if i % 2 else (i - 1) % total_count))

    matrices = jnp.asarray(BUNDLE, bf16)
    message = jax.ShapeDtypeStruct((HALO_ROWS, COARSE), bf16)
    fine = jax.ShapeDtypeStruct((PLANES, ROWS, FINE), bf16)
    own, salinity, wall_index, wall_weight, spacing, matrices = call(
        load_kernel,
        [
            pltpu.VMEM((OWNERS, 4, 384), bf16),
            pltpu.VMEM((PLANES, ROWS, FINE), bf16),
            pltpu.VMEM((BLOCKS, BLOCK), jnp.int32),
            pltpu.VMEM((1, FINE), f32),
            pltpu.VMEM((1, FINE), f32),
            pltpu.VMEM((368, 128), bf16),
        ],
        [ANY] * 6,
        [pltpu.VMEM((3, 2, OWNERS, 4, SLAB), bf16), pltpu.SemaphoreType.DMA((6,))],
        megabytes=56,
    )(velocity, salinity, wall_index.reshape(BLOCKS, BLOCK), wall_weight[None], spacing[None], matrices)
    arrived = lax.all_to_all(own, "wn", split_axis=0, concat_axis=0, tiled=True, axis_index_groups=[ORDER])
    second, first, coarse = call(
        edge_kernel, [message, message, jax.ShapeDtypeStruct((STACK, COARSE), f32)], [VMEM] * 2
    )(salinity, arrived)
    second_in = lax.ppermute(second, ("wn", "sw"), far)
    first_in = lax.ppermute(first, ("wn", "sw"), near)
    inner = call(
        inner_kernel,
        [
            fine,
            jax.ShapeDtypeStruct((5, 16, FINE), f32),
            jax.ShapeDtypeStruct((8, FINE), f32),
            jax.ShapeDtypeStruct((BLOCKS, WINDOW, BLOCK), bf16),
            jax.ShapeDtypeStruct((BLOCKS, BLOCK, WINDOW), bf16),
        ],
        [VMEM] * 6,
        [
            pltpu.VMEM((PLANES, 16, FINE), f32),
            pltpu.VMEM((8, FINE), f32),
            pltpu.VMEM((2 * STACK, COARSE), bf16),
            pltpu.VMEM((2 * STACK, FINE), bf16),
        ],
        cost=pl.CostEstimate(flops=4_000_000_000, bytes_accessed=2_000_000_000, transcendentals=0),
    )(
        salinity, coarse, wall_index, wall_weight, spacing, matrices,
    )
    interior, edges, grouped, hits, turned_hits = inner
    work = [
        pltpu.VMEM((16, COARSE), bf16),
        pltpu.VMEM((16, FINE), f32),
        pltpu.VMEM((16, FINE), bf16),
    ]
    near_updated, sums, near_total = call(
        near_kernel,
        [fine, jax.ShapeDtypeStruct((8, FINE), f32), jax.ShapeDtypeStruct((16, COARSE), f32)],
        [VMEM] * 9,
        work + [pltpu.VMEM((32, FINE), bf16), pltpu.VMEM((BLOCKS, 32, WINDOW), f32)],
        cost=pl.CostEstimate(flops=1000, bytes_accessed=1000, transcendentals=0),
    )(first_in, interior, edges, grouped, hits, turned_hits, wall_index, wall_weight, matrices)
    updated, send = call(
        far_kernel,
        [fine, jax.ShapeDtypeStruct((OWNERS, 4, 128), bf16)],
        [VMEM] * 10,
        work
        + [
            pltpu.VMEM((16, FINE), bf16),
            pltpu.VMEM((BLOCKS, 8, WINDOW), f32),
            pltpu.VMEM((8, COARSE), f32),
            pltpu.VMEM((PLANES, ROWS, FINE), bf16),
            pltpu.SemaphoreType.DMA((PLANES,)),
        ],
        out_specs=[ANY, VMEM],
    )(second_in, near_updated, sums, near_total, edges, hits, turned_hits, wall_index, wall_weight, matrices)
    back = lax.all_to_all(send, "wn", split_axis=0, concat_axis=0, tiled=True, axis_index_groups=[ORDER])
    coarse = call(spread_kernel, jax.ShapeDtypeStruct((2, OWNERS, 4, SLAB), bf16), [VMEM])(back)
    return (updated, coarse)


def solution(mesh):
    in_specs = (P(None, ("wn", "sw"), None), P(None, None, None, "sw", "wn"), P(), P(), P())
    out_specs = (P(None, ("wn", "sw"), None), P(None, None, "sw", "wn"))
    return jax.shard_map(body, mesh=mesh, in_specs=in_specs, out_specs=out_specs, check_vma=False)
```
